256 devices in a mesh: group: 8 (over z_lo, y), fsdp: 32 (over z_hi, x, core).
Axes of the slice: x: 4, y: 4, z: 8 (z_hi: 4, z_lo: 2; z = z_hi * 2 + z_lo), core: 2. Of those that a mesh axis runs over, the one named last changes fastest.
Arguments:
- inner_weights: float32 [8, 2048, 7168], P('group', 'fsdp'), may hold values from -0.125 to 0.125
- inner_grads: bfloat16 [8, 2048, 7168], P('group', 'fsdp'), may hold values from -6 to 6
- first_moment: float32 [8, 2048, 7168], P('group', 'fsdp'), may hold values from -0.6 to 0.6
- second_moment: float32 [8, 2048, 7168], P('group', 'fsdp'), may hold values from 0.01 to 0.25
- anchor: float32 [2048, 7, 1024], P('fsdp'), may hold values from -0.125 to 0.125
- outer_momentum: float32 [2048, 7, 1024], P('fsdp', None, 'group'), may hold values from -0.06 to 0.06
- next_tokens: bfloat16 [49152, 2048], P(('group', 'fsdp')), may hold values from -6 to 6
Outputs:
- preactivations: bfloat16 [49152, 7168], P(('group', 'fsdp'))
- new_anchor: float32 [2048, 7, 1024], P('fsdp', None, 'group')
- new_momentum: float32 [2048, 7, 1024], P('fsdp', None, 'group')
The draws below stay inside these ranges and needn't reach their ends.
All inputs are finite; a program needn't handle non-finite values.
Results may differ from the reference program's by a relative error of at most 0.0049.
Values may be sent and summed in bfloat16 or wider, within the bound.
No kernel may reach another device: no remote copies, remote signals or barrier semaphores. Data moves between devices by JAX's collectives and lax.ppermute only.
A program may use at most 128 MiB of HBM per device.

```python
import math
import jax
import jax.numpy as jnp

D_WIN = 2048
FF_WIN = 7168
SLICES = 7
INNER_STEPS = 100
TOK_DEV = 192
SLICE_W = 1024
GROUPS = 8
TOKENS = 49152
N_FSDP = 32


def shard_levels(rng, extent, shards, least, largest):
    def one(position, blocks):
        heights = jax.random.uniform(jax.random.fold_in(jax.random.fold_in(rng, 6), position), (blocks,), jnp.float32, least / len(shards), largest / len(shards))
        return jnp.repeat(jnp.exp(heights), extent[position] // blocks).reshape((-1,) + (1,) * (len(extent) - position - 1))

    loudness = one(*shards[0])
    for cut in shards[1:]:
        loudness = loudness * one(*cut)
    return loudness


def scatter_about(stream_key, dims, width, limit, split=(), kind=jnp.bfloat16):
    array = width * jax.random.normal(stream_key, dims, jnp.float32)
    if split:
        array = array * shard_levels(stream_key, dims, split, -0.22, 0.18)
    return jnp.clip(array, -limit, limit).astype(kind)


def setup_inputs(seed: int = 0) -> dict:
    splits = jax.random.split(jax.random.key(seed), 8)
    inner_weights = scatter_about(splits[0], (GROUPS, D_WIN, FF_WIN), D_WIN ** -0.5, 0.125, ((0, 8), (1, 32)), jnp.float32)
    inner_grads = scatter_about(splits[1], (GROUPS, D_WIN, FF_WIN), 1.0, 6.0, ((0, 8), (1, 32)))
    first_moment = scatter_about(splits[2], (GROUPS, D_WIN, FF_WIN), 0.1, 0.6, ((0, 8), (1, 32)), jnp.float32)
    second_moment = jnp.clip(jnp.exp(math.log(0.25) - 3.218876 * jax.random.uniform(splits[3], (GROUPS, D_WIN, FF_WIN), jnp.float32) ** shard_levels(splits[3], (GROUPS, D_WIN, FF_WIN), ((0, 8), (1, 32)), -0.2, 0.2)), 0.01, 0.25)
    anchor = scatter_about(splits[4], (D_WIN, SLICES, SLICE_W), D_WIN ** -0.5, 0.125, ((0, 32),), jnp.float32)
    outer_momentum = scatter_about(splits[5], (D_WIN, SLICES, SLICE_W), 0.01, 0.06, ((0, 32), (2, 8)), jnp.float32)
    next_tokens = scatter_about(splits[6], (TOKENS, D_WIN), 1.0, 6.0, ((0, 256),))
    return {"inner_weights": inner_weights, "inner_grads": inner_grads, "first_moment": first_moment, "second_moment": second_moment, "anchor": anchor, "outer_momentum": outer_momentum, "next_tokens": next_tokens}


first_decay = 0.9
second_decay = 0.95
inner_rate = 0.04
weight_decay = 0.1
epsilon = 1e-08
momentum_decay = 0.9
outer_rate = 0.7
mixing = 0.5

def adam_step(weights, gradient, moment_one, moment_two):
    gradient = gradient.astype(jnp.float32)
    first_new = first_decay * moment_one + (1.0 - first_decay) * gradient
    second_new = second_decay * moment_two + (1.0 - second_decay) * gradient * gradient
    correct_one = 1.0 - first_decay ** INNER_STEPS
    correct_two = 1.0 - second_decay ** INNER_STEPS
    update = first_new / correct_one / (jnp.sqrt(second_new / correct_two) + epsilon)
    return weights - inner_rate * (update + weight_decay * weights)

def reference(inner_weights, inner_grads, first_moment, second_moment, anchor, outer_momentum, next_tokens):
    flat_anchor = anchor.reshape(D_WIN, FF_WIN)
    flat_momentum = outer_momentum.reshape(D_WIN, FF_WIN)
    inner_list = []
    summed = jnp.zeros((D_WIN, FF_WIN), jnp.float32)
    for group_index in range(GROUPS):
        inner_new = adam_step(inner_weights[group_index], inner_grads[group_index], first_moment[group_index], second_moment[group_index])
        inner_list.append(inner_new)
        summed = summed + (flat_anchor - inner_new)
    mean_delta = summed / GROUPS
    new_momentum = momentum_decay * flat_momentum + mean_delta
    new_anchor = flat_anchor - outer_rate * (mean_delta + momentum_decay * new_momentum)
    group_rows = TOK_DEV * N_FSDP
    outputs = []
    for group_index in range(GROUPS):
        mixed_weights = (mixing * inner_list[group_index] + (1.0 - mixing) * new_anchor).astype(jnp.bfloat16)
        token_block = next_tokens[group_index * group_rows:(group_index + 1) * group_rows]
        outputs.append(jnp.dot(token_block, mixed_weights, preferred_element_type=jnp.float32).astype(jnp.bfloat16))
    preactivations = jnp.concatenate(outputs, axis=0)
    return (preactivations, new_anchor.reshape(D_WIN, SLICES, SLICE_W), new_momentum.reshape(D_WIN, SLICES, SLICE_W))
```

```python
import jax
import jax.numpy as jnp
from jax import lax
from jax.experimental import pallas as pl
from jax.experimental.pallas import tpu as pltpu
from jax.sharding import Mesh
from jax.sharding import PartitionSpec as P

INNER_STEPS = 100

first_decay = 0.9
second_decay = 0.95
inner_rate = 0.04
weight_decay = 0.1
epsilon = 1e-08
momentum_decay = 0.9
outer_rate = 0.7
mixing = 0.5

GROUP = ("zl", "y")
ROWS = ("zh", "x", "c")
PLANE = ("x", "c")
SLICES = 7
LANES = 128
CHUNKS = ((0, 4), (4, 7))
BRIEF = pl.CostEstimate(flops=1, bytes_accessed=1, transcendentals=0)


def adam_step(weights, gradient, moment_one, moment_two):
    gradient = gradient.astype(jnp.float32)
    first_new = first_decay * moment_one + (1.0 - first_decay) * gradient
    second_new = second_decay * moment_two + (1.0 - second_decay) * gradient * gradient
    correct_one = 1.0 - first_decay**INNER_STEPS
    correct_two = 1.0 - second_decay**INNER_STEPS
    update = first_new / correct_one / (jnp.sqrt(second_new / correct_two) + epsilon)
    return weights - inner_rate * (update + weight_decay * weights)


def inner_kernel(weights, grads, moment_one, moment_two, anchor, pieces):
    inner_new = adam_step(weights[...], grads[...], moment_one[...], moment_two[...])
    pseudo = (anchor[0] - inner_new).astype(jnp.bfloat16)
    for g in range(pieces.shape[0]):
        pieces[g] = pseudo[:, g * LANES : (g + 1) * LANES]


def inner_step(weights, grads, moment_one, moment_two, anchor, groups):
    rows, width = weights.shape[0], anchor.shape[2]
    wide = pl.BlockSpec((rows, width), lambda s: (0, s))
    return pl.pallas_call(
        inner_kernel,
        grid=(SLICES,),
        in_specs=[wide] * 4 + [pl.BlockSpec((1, rows, width), lambda s: (s, 0, 0))],
        out_specs=pl.BlockSpec((groups, rows, LANES), lambda s: (0, 0, s)),
        out_shape=jax.ShapeDtypeStruct((groups, rows, SLICES * LANES), jnp.bfloat16),
        compiler_params=pltpu.CompilerParams(vmem_limit_bytes=60 * 1024 * 1024),
        cost_estimate=BRIEF,
    )(weights, grads, moment_one, moment_two, anchor)


def outer_kernel(place, pieces, anchor, momentum, anchor_new, momentum_new, *mixed):
    groups = pieces.shape[0]
    pseudo = [pieces[g].astype(jnp.float32) for g in range(groups)]
    mean_delta = sum(pseudo[1:], pseudo[0]) / groups
    after = momentum_decay * momentum[0] + mean_delta
    moved = anchor[0] - outer_rate * (mean_delta + momentum_decay * after)
    momentum_new[0] = after
    anchor_new[0] = moved
    s = pl.program_id(0)
    for (first, last), part in zip(CHUNKS, mixed):

        @pl.when((s >= first) & (s < last))
        def _():
            for g in range(groups):
                inner_new = anchor[0] - pseudo[g]
                part[g] = (mixing * inner_new + (1.0 - mixing) * moved).astype(jnp.bfloat16)


def outer_step(place, pieces, anchor, momentum):
    groups, rows, _ = pieces.shape
    part = pl.BlockSpec((1, rows, LANES), lambda s, p: (s, 0, 0))
    anchor_part = pl.BlockSpec((1, rows, LANES), lambda s, p: (s, 0, p[0]))
    new = jax.ShapeDtypeStruct(momentum.shape, jnp.float32)

    def chunk(first, last):
        return pl.BlockSpec(
            (groups, rows, LANES), lambda s, p: (0, 0, jnp.clip(s - first, 0, last - first - 1))
        )

    return pl.pallas_call(
        outer_kernel,
        grid_spec=pltpu.PrefetchScalarGridSpec(
            num_scalar_prefetch=1,
            grid=(SLICES,),
            in_specs=[pl.BlockSpec((groups, rows, LANES), lambda s, p: (0, 0, s)), anchor_part, part],
            out_specs=[part, part] + [chunk(*c) for c in CHUNKS],
        ),
        out_shape=[new, new]
        + [
            jax.ShapeDtypeStruct((groups, rows, (last - first) * LANES), jnp.bfloat16)
            for first, last in CHUNKS
        ],
        cost_estimate=BRIEF,
    )(place, pieces, anchor, momentum)


def product_kernel(place, tokens, *refs):
    *weights, out = refs
    total = None
    for k, weight in enumerate(weights):
        depth = weight.shape[0]
        columns = pl.ds(pl.multiple_of(place[2 + k], depth), depth)
        term = jnp.dot(tokens[0, :, columns], weight[...], preferred_element_type=jnp.float32)
        total = term if total is None else total + term
    chips = out.shape[1]
    total = total.astype(jnp.bfloat16).reshape(chips, -1, out.shape[3])
    for k, step in enumerate((0, 3, 1, 2)):
        out[0, lax.rem(place[0] + step, chips)] = total[k]


def product(place, tokens, weights, cost):
    cores, rows, depth = tokens.shape
    chips = 4
    width = weights[0].shape[1]
    return pl.pallas_call(
        product_kernel,
        grid_spec=pltpu.PrefetchScalarGridSpec(
            num_scalar_prefetch=1,
            grid=(cores,),
            in_specs=[pl.BlockSpec((1, rows, depth), lambda d, p: (d, 0, 0))]
            + [pl.BlockSpec(w.shape, lambda d, p: (0, 0)) for w in weights],
            out_specs=pl.BlockSpec(
                (1, chips, rows // chips, width), lambda d, p: (p[1] ^ d, 0, 0, 0)
            ),
        ),
        out_shape=jax.ShapeDtypeStruct((cores, chips, rows // chips, width), jnp.bfloat16),
        compiler_params=pltpu.CompilerParams(vmem_limit_bytes=48 * 1024 * 1024),
        cost_estimate=cost,
    )(place, tokens, *weights)


def assemble_kernel(part, *refs):
    out = refs[-1]
    half = part.shape[0] // 2
    for j in range(2 * half):
        column = (2 * (j % half) + j // half) * LANES
        out[:, column : column + LANES] = part[j]


def assemble(part, whole, first, last):
    count, rows, _ = part.shape
    width = count * LANES
    held = [] if whole is None else [whole]
    return pl.pallas_call(
        assemble_kernel,
        grid=(last - first,),
        in_specs=[pl.BlockSpec((count, rows, LANES), lambda s: (0, 0, s))]
        + [pl.BlockSpec(memory_space=pl.ANY)] * len(held),
        out_specs=pl.BlockSpec((rows, width), lambda s: (0, s + first)),
        out_shape=jax.ShapeDtypeStruct((rows, SLICES * width), jnp.bfloat16),
        input_output_aliases={1: 0} if held else {},
        cost_estimate=BRIEF,
    )(part, *held)


def shift(array, axis, k):
    n = lax.axis_size(axis)
    return lax.ppermute(array, axis, [(i, (i + k) % n) for i in range(n)])


def neighbours(array, axis):
    return shift(array, axis, 1), shift(array, axis, -1)


def opposite(low, high, axis):
    half = low.shape[0] // 2
    return shift(low[:half], axis, 1), shift(high[half:], axis, -1)


def after(array, earlier):
    if earlier is None:
        return array
    return lax.optimization_barrier((array, earlier))[0]


def body(
    inner_weights, inner_grads, first_moment, second_moment, anchor, outer_momentum, next_tokens
):
    groups = lax.axis_size(GROUP)
    place = lax.axis_index(GROUP).astype(jnp.int32).reshape(1)
    deep = next_tokens.shape[1] // lax.axis_size("zh")
    z = [(lax.axis_index("zh") + k) % lax.axis_size("zh") * deep for k in (0, -1, 1, 2, 2)]
    z[4] = z[4] + deep // 2
    spot = jnp.stack([lax.axis_index("x"), lax.axis_index("c")] + z).astype(jnp.int32)
    anchor = anchor.transpose(1, 0, 2)
    momentum = outer_momentum.transpose(1, 0, 2)

    pieces = inner_step(
        inner_weights[0], inner_grads[0], first_moment[0], second_moment[0], anchor, groups
    )
    pieces = lax.all_to_all(pieces, GROUP, 0, 0, tiled=True)
    sides = neighbours(next_tokens, "x")
    anchor_new, momentum_new, *mixed = outer_step(place, after(pieces, sides), anchor, momentum)
    across = opposite(*sides, "x")

    weights, held = [], across
    for part in mixed:
        part = lax.all_to_all(part, GROUP, 0, 0, tiled=True)
        part = lax.all_to_all(after(part, held), PLANE, 0, 0, tiled=True)
        block = part.reshape(-1, part.shape[2])
        held = neighbours(block, "zh")
        weights.append((block, *held, *opposite(*held, "zh")))

    near = jnp.concatenate([next_tokens, *sides, *across])
    tokens = jnp.stack([near, shift(near, "c", 1)])
    preactivations = None
    for (first, last), weight in zip(CHUNKS, weights):
        out = product(spot, tokens, weight, BRIEF)
        out = out.reshape((-1,) + out.shape[2:])
        part = lax.all_to_all(out, ("c", "x"), 0, 0, tiled=True)
        preactivations = assemble(part, preactivations, first, last)
    anchor_new = anchor_new.transpose(1, 0, 2)
    momentum_new = momentum_new.transpose(1, 0, 2)
    return (preactivations, anchor_new, momentum_new)


def solution(mesh):
    fine = Mesh(mesh.devices.reshape(2, 4, 4, 4, 2), GROUP + ROWS)
    shard = P(GROUP, ROWS, None)
    in_specs = (
        shard,
        shard,
        shard,
        shard,
        P(ROWS, None, None),
        P(ROWS, None, GROUP),
        P(GROUP + ROWS, None),
    )
    out_specs = (P(GROUP + ROWS, None), P(ROWS, None, GROUP), P(ROWS, None, GROUP))
    return jax.shard_map(body, mesh=fine, in_specs=in_specs, out_specs=out_specs, check_vma=False)
```

```python
import functools

import jax
import jax.numpy as jnp
from jax import lax
from jax.experimental import pallas as pl
from jax.experimental.pallas import tpu as pltpu
from jax.sharding import Mesh
from jax.sharding import PartitionSpec as P

INNER_STEPS = 100

first_decay = 0.9
second_decay = 0.95
inner_rate = 0.04
weight_decay = 0.1
epsilon = 1e-08
momentum_decay = 0.9
outer_rate = 0.7
mixing = 0.5

GROUP = ("zl", "y")
ROWS = ("zh", "x", "c")
PLANE = ("x", "c")
SLICES = 7
LANES = 128
CUT = 4
STRIP = 4
WHOLE = pl.BlockSpec(memory_space=pltpu.VMEM)
ANYWHERE = pl.BlockSpec(memory_space=pl.ANY)
LARGE = pltpu.CompilerParams(vmem_limit_bytes=59 * 1024 * 1024)
BRIEF = pl.CostEstimate(flops=1, bytes_accessed=1, transcendentals=0)


def pseudo_gradient(weights, gradient, moment_one, moment_two, anchor):
    gradient = gradient.astype(jnp.float32)
    correct_one = 1.0 - first_decay**INNER_STEPS
    correct_two = 1.0 - second_decay**INNER_STEPS
    scale = inner_rate / correct_one
    first_new = (scale * first_decay) * moment_one + (scale * (1.0 - first_decay)) * gradient
    second_new = (second_decay / correct_two) * moment_two
    second_new = second_new + ((1.0 - second_decay) / correct_two) * (gradient * gradient)
    root = second_new * lax.rsqrt(second_new)
    step = first_new / (root + epsilon)
    return (anchor - (1.0 - inner_rate * weight_decay) * weights) + step


def inner_kernel(place, weights, grads, moment_one, moment_two, anchor, *refs):
    pieces, anchor_part, *held, arrived = refs
    slices, _, width = anchor.shape

    def parts(s):
        lanes = pl.ds(s * width, width)
        sources = [r.at[:, lanes] for r in (weights, grads, moment_one, moment_two)]
        return [
            pltpu.make_async_copy(source, into.at[s], arrived.at[s, i])
            for i, (source, into) in enumerate(zip(sources + [anchor.at[s]], held))
        ]

    copies = [parts(s) for s in range(slices)]
    for copy in sum(copies, []):
        copy.start()
    mine = pl.ds(pl.multiple_of(place[0] * LANES, LANES), LANES)
    for s in range(slices):
        for copy in copies[s]:
            copy.wait()
        pseudo = pseudo_gradient(*[h[s] for h in held]).astype(jnp.bfloat16)
        for g in range(pieces.shape[0]):
            pieces[g, :, s * LANES : (s + 1) * LANES] = pseudo[:, g * LANES : (g + 1) * LANES]
        anchor_part[s] = held[4][s, :, mine]


def inner_step(place, weights, grads, moment_one, moment_two, anchor, groups):
    slices, rows, _ = anchor.shape
    wide = pltpu.VMEM(anchor.shape, jnp.float32)
    return pl.pallas_call(
        inner_kernel,
        in_specs=[pl.BlockSpec(memory_space=pltpu.SMEM)] + [ANYWHERE] * 5,
        out_specs=[WHOLE] * 2,
        out_shape=[
            jax.ShapeDtypeStruct((groups, rows, slices * LANES), jnp.bfloat16),
            jax.ShapeDtypeStruct((slices, rows, LANES), jnp.float32),
        ],
        scratch_shapes=[wide, pltpu.VMEM(anchor.shape, jnp.bfloat16), wide, wide, wide]
        + [pltpu.SemaphoreType.DMA((slices, 5))],
        compiler_params=LARGE,
        cost_estimate=BRIEF,
    )(place, weights, grads, moment_one, moment_two, anchor)


def outer_kernel(pieces, anchor, momentum, anchor_new, momentum_new, mixed):
    groups = pieces.shape[0]
    for s in range(anchor.shape[0]):
        lanes = slice(s * LANES, (s + 1) * LANES)
        old = anchor[s]
        pseudo = [pieces[g, :, lanes].astype(jnp.float32) for g in range(groups)]
        mean_delta = sum(pseudo[1:], pseudo[0]) / groups
        after = momentum_decay * momentum[s] + mean_delta
        moved = old - outer_rate * (mean_delta + momentum_decay * after)
        momentum_new[s] = after
        anchor_new[s] = moved
        for g in range(groups):
            inner_new = old - pseudo[g]
            mixed[g, :, lanes] = (mixing * inner_new + (1.0 - mixing) * moved).astype(jnp.bfloat16)


def outer_step(pieces, anchor_part, momentum):
    new = jax.ShapeDtypeStruct(anchor_part.shape, jnp.float32)
    return pl.pallas_call(
        outer_kernel,
        in_specs=[WHOLE] * 3,
        out_specs=[WHOLE] * 3,
        out_shape=[new, new, jax.ShapeDtypeStruct(pieces.shape, jnp.bfloat16)],
        compiler_params=LARGE,
        cost_estimate=BRIEF,
    )(pieces, anchor_part, momentum)


def product_kernel(place, tokens, *refs):
    *weights, out = refs
    depth = weights[0].shape[0]
    total = None
    for k, weight in enumerate(weights):
        columns = pl.ds(pl.multiple_of(place[k], depth), depth)
        term = jnp.dot(tokens[:, columns], weight[...], preferred_element_type=jnp.float32)
        total = term if total is None else total + term
    out[...] = total.astype(jnp.bfloat16).reshape(out.shape)


def product(place, tokens, weights, pieces):
    rows, depth = tokens.shape
    width = weights[0].shape[1]
    return pl.pallas_call(
        product_kernel,
        grid_spec=pltpu.PrefetchScalarGridSpec(
            num_scalar_prefetch=1,
            grid=(pieces // STRIP,),
            in_specs=[pl.BlockSpec((STRIP * rows // pieces, depth), lambda i, p: (i, 0))]
            + [WHOLE] * len(weights),
            out_specs=pl.BlockSpec((STRIP, rows // pieces, width), lambda i, p: (i, 0, 0)),
        ),
        out_shape=jax.ShapeDtypeStruct((pieces, rows // pieces, width), jnp.bfloat16),
        compiler_params=pltpu.CompilerParams(vmem_limit_bytes=55 * 1024 * 1024),
        cost_estimate=BRIEF,
    )(place, tokens, *weights)


def assemble_kernel(first, part, *refs):
    out, left = refs[-2:]
    count, _, width = part.shape
    sent = []
    for j in range(count):
        for s in range(width // LANES):
            column = (first + s) * count + j
            sent.append(
                pltpu.make_async_copy(
                    part.at[j, :, pl.ds(s * LANES, LANES)],
                    out.at[:, pl.ds(column * LANES, LANES)],
                    left.at[j, s],
                )
            )
    for copy in sent:
        copy.start()
    for copy in sent:
        copy.wait()


def assemble(part, whole, first):
    count, rows, width = part.shape
    held = [] if whole is None else [whole]
    return pl.pallas_call(
        functools.partial(assemble_kernel, first),
        in_specs=[WHOLE] + [ANYWHERE] * len(held),
        out_specs=ANYWHERE,
        out_shape=jax.ShapeDtypeStruct((rows, SLICES * count * LANES), jnp.bfloat16),
        scratch_shapes=[pltpu.SemaphoreType.DMA((count, width // LANES))],
        input_output_aliases={1: 0} if held else {},
        compiler_params=pltpu.CompilerParams(vmem_limit_bytes=16 * 1024 * 1024),
        cost_estimate=BRIEF,
    )(part, *held)


def ring(array, axis):
    n = lax.axis_size(axis)
    pairs = [(2 * i + c, 2 * ((i + 1 - 2 * c) % n) + c) for i in range(n) for c in (0, 1)]
    return lax.ppermute(array, (axis, "c"), pairs)


def rings(block):
    blocks = [block]
    for _ in range(lax.axis_size("zh") - 1):
        blocks.append(ring(blocks[-1], "zh"))
    return blocks


def after(array, *earlier):
    return lax.optimization_barrier((array, earlier))[0]


def body(
    inner_weights, inner_grads, first_moment, second_moment, anchor, outer_momentum, next_tokens
):
    groups = lax.axis_size(GROUP)
    place = lax.axis_index(GROUP).astype(jnp.int32).reshape(1)
    turn = 2 * lax.axis_index("c") - 1
    deep = next_tokens.shape[1] // lax.axis_size("zh")
    spot = [
        (lax.axis_index("zh") + turn * k) % lax.axis_size("zh") * deep + half
        for half in (0, deep // 2)
        for k in range(4)
    ]
    spot = jnp.stack(spot).astype(jnp.int32)
    anchor = anchor.transpose(1, 0, 2)
    momentum = outer_momentum.transpose(1, 0, 2)
    state = (inner_weights[0], inner_grads[0], first_moment[0], second_moment[0], anchor)

    pieces, anchor_part = inner_step(place, *state, groups)
    pieces = lax.all_to_all(pieces, GROUP, 0, 0, tiled=True)
    anchor_new, momentum_new, mixed = outer_step(pieces, anchor_part, momentum)
    tokens = lax.all_gather(next_tokens, PLANE, axis=0, tiled=True)
    mixed = lax.all_to_all(mixed, GROUP, 0, 0, tiled=True)
    mixed = lax.all_to_all(mixed, PLANE, 0, 0, tiled=True)
    block = mixed.reshape(-1, mixed.shape[2])
    half = block.shape[0] // 2
    low, high = block[:half], block[half:]
    cut = CUT * LANES
    low_a, high_a = rings(low[:, :cut]), rings(high[:, :cut])
    low_b, high_b = rings(after(low[:, cut:], low_a)), rings(after(high[:, cut:], high_a))
    out_a = product(spot, tokens, low_a + high_a, lax.axis_size(PLANE))
    out_a = after(out_a, low_b[1], high_b[1])
    part_a = lax.all_to_all(out_a, PLANE, 0, 0, tiled=True)
    out_b = product(spot, tokens, low_b + high_b, lax.axis_size(PLANE))
    part_b = lax.all_to_all(out_b, PLANE, 0, 0, tiled=True)
    preactivations = assemble(part_a, None, 0)
    preactivations = assemble(part_b, preactivations, CUT)
    return (preactivations, anchor_new.transpose(1, 0, 2), momentum_new.transpose(1, 0, 2))


def solution(mesh):
    fine = Mesh(mesh.devices.reshape(2, 4, 4, 4, 2), GROUP + ROWS)
    shard = P(GROUP, ROWS, None)
    in_specs = (
        shard,
        shard,
        shard,
        shard,
        P(ROWS, None, None),
        P(ROWS, None, GROUP),
        P(GROUP + ROWS, None),
    )
    out_specs = (P(GROUP + ROWS, None), P(ROWS, None, GROUP), P(ROWS, None, GROUP))
    return jax.shard_map(body, mesh=fine, in_specs=in_specs, out_specs=out_specs, check_vma=False)
```

```python
import functools

import jax
import jax.numpy as jnp
from jax import lax
from jax.experimental import pallas as pl
from jax.experimental.pallas import tpu as pltpu
from jax.sharding import Mesh
from jax.sharding import PartitionSpec as P

INNER_STEPS = 100

first_decay = 0.9
second_decay = 0.95
inner_rate = 0.04
weight_decay = 0.1
epsilon = 1e-08
momentum_decay = 0.9
outer_rate = 0.7
mixing = 0.5

GROUP = ("zl", "y")
ROWS = ("zh", "x", "c")
PLANE = ("x", "c")
SLICES = 7
LANES = 128
CUT = 5
STRIP = 4
WHOLE = pl.BlockSpec(memory_space=pltpu.VMEM)
ANYWHERE = pl.BlockSpec(memory_space=pl.ANY)
LARGE = pltpu.CompilerParams(vmem_limit_bytes=59 * 1024 * 1024)
BRIEF = pl.CostEstimate(flops=1, bytes_accessed=1, transcendentals=0)


def pseudo_gradient(weights, gradient, moment_one, moment_two, anchor):
    gradient = gradient.astype(jnp.float32)
    correct_one = 1.0 - first_decay**INNER_STEPS
    correct_two = 1.0 - second_decay**INNER_STEPS
    scale = inner_rate / correct_one
    first_new = (scale * first_decay) * moment_one + (scale * (1.0 - first_decay)) * gradient
    second_new = (second_decay / correct_two) * moment_two
    second_new = second_new + ((1.0 - second_decay) / correct_two) * (gradient * gradient)
    root = second_new * lax.rsqrt(second_new)
    step = first_new / (root + epsilon)
    return (anchor - (1.0 - inner_rate * weight_decay) * weights) + step


def inner_kernel(place, weights, grads, moment_one, moment_two, anchor, *refs):
    pieces, anchor_part, *held, arrived = refs
    slices, _, width = anchor.shape

    def parts(s):
        lanes = pl.ds(s * width, width)
        sources = [r.at[:, lanes] for r in (weights, grads, moment_one, moment_two)]
        return [
            pltpu.make_async_copy(source, into.at[s], arrived.at[s, i])
            for i, (source, into) in enumerate(zip(sources + [anchor.at[s]], held))
        ]

    copies = [parts(s) for s in range(slices)]
    for copy in sum(copies, []):
        copy.start()
    mine = pl.ds(pl.multiple_of(place[0] * LANES, LANES), LANES)
    for s in range(slices):
        for copy in copies[s]:
            copy.wait()
        pseudo = pseudo_gradient(*[h[s] for h in held]).astype(jnp.bfloat16)
        for g in range(pieces.shape[0]):
            pieces[g, :, s * LANES : (s + 1) * LANES] = pseudo[:, g * LANES : (g + 1) * LANES]
        anchor_part[s] = held[4][s, :, mine]


def inner_step(place, weights, grads, moment_one, moment_two, anchor, groups):
    slices, rows, _ = anchor.shape
    wide = pltpu.VMEM(anchor.shape, jnp.float32)
    return pl.pallas_call(
        inner_kernel,
        in_specs=[pl.BlockSpec(memory_space=pltpu.SMEM)] + [ANYWHERE] * 5,
        out_specs=[WHOLE] * 2,
        out_shape=[
            jax.ShapeDtypeStruct((groups, rows, slices * LANES), jnp.bfloat16),
            jax.ShapeDtypeStruct((slices, rows, LANES), jnp.float32),
        ],
        scratch_shapes=[wide, pltpu.VMEM(anchor.shape, jnp.bfloat16), wide, wide, wide]
        + [pltpu.SemaphoreType.DMA((slices, 5))],
        compiler_params=LARGE,
        cost_estimate=BRIEF,
    )(place, weights, grads, moment_one, moment_two, anchor)


def outer_kernel(pieces, anchor, momentum, anchor_new, momentum_new, mixed):
    groups = pieces.shape[0]
    for s in range(anchor.shape[0]):
        lanes = slice(s * LANES, (s + 1) * LANES)
        old = anchor[s]
        pseudo = [pieces[g, :, lanes].astype(jnp.float32) for g in range(groups)]
        mean_delta = sum(pseudo[1:], pseudo[0]) / groups
        after = momentum_decay * momentum[s] + mean_delta
        moved = old - outer_rate * (mean_delta + momentum_decay * after)
        momentum_new[s] = after
        anchor_new[s] = moved
        for g in range(groups):
            inner_new = old - pseudo[g]
            mixed[g, :, lanes] = (mixing * inner_new + (1.0 - mixing) * moved).astype(jnp.bfloat16)


def outer_step(pieces, anchor_part, momentum):
    new = jax.ShapeDtypeStruct(anchor_part.shape, jnp.float32)
    return pl.pallas_call(
        outer_kernel,
        in_specs=[WHOLE] * 3,
        out_specs=[WHOLE] * 3,
        out_shape=[new, new, jax.ShapeDtypeStruct(pieces.shape, jnp.bfloat16)],
        compiler_params=LARGE,
        cost_estimate=BRIEF,
    )(pieces, anchor_part, momentum)


def product_kernel(place, tokens, *refs):
    *weights, out = refs
    depth = weights[0].shape[0]
    total = None
    for k, weight in enumerate(weights):
        columns = pl.ds(pl.multiple_of(place[k], depth), depth)
        term = jnp.dot(tokens[:, columns], weight[...], preferred_element_type=jnp.float32)
        total = term if total is None else total + term
    out[...] = total.astype(jnp.bfloat16).reshape(out.shape)


def product(place, tokens, weights, pieces):
    rows, depth = tokens.shape
    width = weights[0].shape[1]
    return pl.pallas_call(
        product_kernel,
        grid_spec=pltpu.PrefetchScalarGridSpec(
            num_scalar_prefetch=1,
            grid=(pieces // STRIP,),
            in_specs=[pl.BlockSpec((STRIP * rows // pieces, depth), lambda i, p: (i, 0))]
            + [WHOLE] * len(weights),
            out_specs=pl.BlockSpec((STRIP, rows // pieces, width), lambda i, p: (i, 0, 0)),
        ),
        out_shape=jax.ShapeDtypeStruct((pieces, rows // pieces, width), jnp.bfloat16),
        compiler_params=pltpu.CompilerParams(vmem_limit_bytes=55 * 1024 * 1024),
        cost_estimate=BRIEF,
    )(place, tokens, *weights)


def assemble_kernel(first, part, *refs):
    out, left = refs[-2:]
    count, _, width = part.shape
    sent = []
    for j in range(count):
        for s in range(width // LANES):
            column = (first + s) * count + j
            sent.append(
                pltpu.make_async_copy(
                    part.at[j, :, pl.ds(s * LANES, LANES)],
                    out.at[:, pl.ds(column * LANES, LANES)],
                    left.at[j, s],
                )
            )
    for copy in sent:
        copy.start()
    for copy in sent:
        copy.wait()


def assemble(part, whole, first):
    count, rows, width = part.shape
    held = [] if whole is None else [whole]
    return pl.pallas_call(
        functools.partial(assemble_kernel, first),
        in_specs=[WHOLE] + [ANYWHERE] * len(held),
        out_specs=ANYWHERE,
        out_shape=jax.ShapeDtypeStruct((rows, SLICES * count * LANES), jnp.bfloat16),
        scratch_shapes=[pltpu.SemaphoreType.DMA((count, width // LANES))],
        input_output_aliases={1: 0} if held else {},
        compiler_params=pltpu.CompilerParams(vmem_limit_bytes=16 * 1024 * 1024),
        cost_estimate=BRIEF,
    )(part, *held)


def ring(array, axis):
    n = lax.axis_size(axis)
    pairs = [(2 * i + c, 2 * ((i + 1 - 2 * c) % n) + c) for i in range(n) for c in (0, 1)]
    return lax.ppermute(array, (axis, "c"), pairs)


def rings(block):
    blocks = [block]
    for _ in range(lax.axis_size("zh") - 1):
        blocks.append(ring(blocks[-1], "zh"))
    return blocks


def after(array, *earlier):
    return lax.optimization_barrier((array, earlier))[0]


def body(
    inner_weights, inner_grads, first_moment, second_moment, anchor, outer_momentum, next_tokens
):
    groups = lax.axis_size(GROUP)
    place = lax.axis_index(GROUP).astype(jnp.int32).reshape(1)
    turn = 2 * lax.axis_index("c") - 1
    deep = next_tokens.shape[1] // lax.axis_size("zh")
    spot = [
        (lax.axis_index("zh") + turn * k) % lax.axis_size("zh") * deep + half
        for half in (0, deep // 2)
        for k in range(4)
    ]
    spot = jnp.stack(spot).astype(jnp.int32)
    anchor = anchor.transpose(1, 0, 2)
    momentum = outer_momentum.transpose(1, 0, 2)
    state = (inner_weights[0], inner_grads[0], first_moment[0], second_moment[0], anchor)

    pieces, anchor_part = inner_step(place, *state, groups)
    pieces = lax.all_to_all(pieces, GROUP, 0, 0, tiled=True)
    anchor_new, momentum_new, mixed = outer_step(pieces, anchor_part, momentum)
    tokens = lax.all_gather(next_tokens, PLANE, axis=0, tiled=True)
    mixed = lax.all_to_all(mixed, GROUP, 0, 0, tiled=True)
    mixed = lax.all_to_all(mixed, PLANE, 0, 0, tiled=True)
    block = mixed.reshape(-1, mixed.shape[2])
    half = block.shape[0] // 2
    low, high = block[:half], block[half:]
    cut = CUT * LANES
    low_a, high_a = rings(low[:, :cut]), rings(high[:, :cut])
    low_b, high_b = rings(after(low[:, cut:], low_a[:3])), rings(after(high[:, cut:], high_a[:3]))
    out_a = product(spot, tokens, low_a + high_a, lax.axis_size(PLANE))
    out_a = after(out_a, low_b[1], high_b[1])
    part_a = lax.all_to_all(out_a, PLANE, 0, 0, tiled=True)
    out_b = product(spot, tokens, low_b + high_b, lax.axis_size(PLANE))
    part_b = lax.all_to_all(out_b, PLANE, 0, 0, tiled=True)
    preactivations = assemble(part_a, None, 0)
    preactivations = assemble(part_b, preactivations, CUT)
    return (preactivations, anchor_new.transpose(1, 0, 2), momentum_new.transpose(1, 0, 2))


def solution(mesh):
    fine = Mesh(mesh.devices.reshape(2, 4, 4, 4, 2), GROUP + ROWS)
    shard = P(GROUP, ROWS, None)
    in_specs = (
        shard,
        shard,
        shard,
        shard,
        P(ROWS, None, None),
        P(ROWS, None, GROUP),
        P(GROUP + ROWS, None),
    )
    out_specs = (P(GROUP + ROWS, None), P(ROWS, None, GROUP), P(ROWS, None, GROUP))
    return jax.shard_map(body, mesh=fine, in_specs=in_specs, out_specs=out_specs, check_vma=False)
```

```python
import functools

import jax
import jax.numpy as jnp
from jax import lax
from jax.experimental import pallas as pl
from jax.experimental.pallas import tpu as pltpu
from jax.sharding import Mesh
from jax.sharding import PartitionSpec as P

INNER_STEPS = 100

first_decay = 0.9
second_decay = 0.95
inner_rate = 0.04
weight_decay = 0.1
epsilon = 1e-08
momentum_decay = 0.9
outer_rate = 0.7
mixing = 0.5

GROUP = ("zl", "y")
ROWS = ("zh", "x", "c")
PLANE = ("x", "c")
SLICES = 7
LANES = 128
CUT = 5
WHOLE = pl.BlockSpec(memory_space=pltpu.VMEM)
ANYWHERE = pl.BlockSpec(memory_space=pl.ANY)
LARGE = pltpu.CompilerParams(vmem_limit_bytes=59 * 1024 * 1024)
BRIEF = pl.CostEstimate(flops=1, bytes_accessed=1, transcendentals=0)


def pseudo_gradient(weights, gradient, moment_one, moment_two, anchor):
    gradient = gradient.astype(jnp.float32)
    correct_one = 1.0 - first_decay**INNER_STEPS
    correct_two = 1.0 - second_decay**INNER_STEPS
    scale = inner_rate / correct_one
    first_new = (scale * first_decay) * moment_one + (scale * (1.0 - first_decay)) * gradient
    second_new = (second_decay / correct_two) * moment_two
    second_new = second_new + ((1.0 - second_decay) / correct_two) * (gradient * gradient)
    root = second_new * lax.rsqrt(second_new)
    step = first_new / (root + epsilon)
    return (anchor - (1.0 - inner_rate * weight_decay) * weights) + step


def inner_kernel(place, weights, grads, moment_one, moment_two, anchor, *refs):
    pieces, anchor_part, *held, arrived = refs
    slices, _, width = anchor.shape

    def parts(s):
        lanes = pl.ds(s * width, width)
        sources = [r.at[:, lanes] for r in (weights, grads, moment_one, moment_two)]
        return [
            pltpu.make_async_copy(source, into.at[s], arrived.at[s, i])
            for i, (source, into) in enumerate(zip(sources + [anchor.at[s]], held))
        ]

    copies = [parts(s) for s in range(slices)]
    for copy in sum(copies, []):
        copy.start()
    mine = pl.ds(pl.multiple_of(place[0] * LANES, LANES), LANES)
    for s in range(slices):
        for copy in copies[s]:
            copy.wait()
        pseudo = pseudo_gradient(*[h[s] for h in held]).astype(jnp.bfloat16)
        for g in range(pieces.shape[0]):
            pieces[g, :, s * LANES : (s + 1) * LANES] = pseudo[:, g * LANES : (g + 1) * LANES]
        anchor_part[s] = held[4][s, :, mine]


def inner_step(place, weights, grads, moment_one, moment_two, anchor, groups):
    slices, rows, _ = anchor.shape
    wide = pltpu.VMEM(anchor.shape, jnp.float32)
    return pl.pallas_call(
        inner_kernel,
        in_specs=[pl.BlockSpec(memory_space=pltpu.SMEM)] + [ANYWHERE] * 5,
        out_specs=[WHOLE] * 2,
        out_shape=[
            jax.ShapeDtypeStruct((groups, rows, slices * LANES), jnp.bfloat16),
            jax.ShapeDtypeStruct((slices, rows, LANES), jnp.float32),
        ],
        scratch_shapes=[wide, pltpu.VMEM(anchor.shape, jnp.bfloat16), wide, wide, wide]
        + [pltpu.SemaphoreType.DMA((slices, 5))],
        compiler_params=LARGE,
        cost_estimate=BRIEF,
    )(place, weights, grads, moment_one, moment_two, anchor)


def outer_kernel(pieces, anchor, momentum, anchor_new, momentum_new, mixed):
    groups = pieces.shape[0]
    for s in range(anchor.shape[0]):
        lanes = slice(s * LANES, (s + 1) * LANES)
        old = anchor[s]
        pseudo = [pieces[g, :, lanes].astype(jnp.float32) for g in range(groups)]
        mean_delta = sum(pseudo[1:], pseudo[0]) / groups
        after = momentum_decay * momentum[s] + mean_delta
        moved = old - outer_rate * (mean_delta + momentum_decay * after)
        momentum_new[s] = after
        anchor_new[s] = moved
        for g in range(groups):
            inner_new = old - pseudo[g]
            mixed[g, :, lanes] = (mixing * inner_new + (1.0 - mixing) * moved).astype(jnp.bfloat16)


def outer_step(pieces, anchor_part, momentum):
    new = jax.ShapeDtypeStruct(anchor_part.shape, jnp.float32)
    return pl.pallas_call(
        outer_kernel,
        in_specs=[WHOLE] * 3,
        out_specs=[WHOLE] * 3,
        out_shape=[new, new, jax.ShapeDtypeStruct(pieces.shape, jnp.bfloat16)],
        compiler_params=LARGE,
        cost_estimate=BRIEF,
    )(pieces, anchor_part, momentum)


def product_kernel(place, tokens, *refs):
    *weights, out = refs
    depth = weights[0].shape[0]
    total = None
    for k, weight in enumerate(weights):
        columns = pl.ds(pl.multiple_of(place[k], depth), depth)
        term = jnp.dot(tokens[:, columns], weight[...], preferred_element_type=jnp.float32)
        total = term if total is None else total + term
    out[...] = total.astype(jnp.bfloat16).reshape(out.shape)


def product(place, tokens, weights, pieces, strip):
    rows, depth = tokens.shape
    width = weights[0].shape[1]
    return pl.pallas_call(
        product_kernel,
        grid_spec=pltpu.PrefetchScalarGridSpec(
            num_scalar_prefetch=1,
            grid=(pieces // strip,),
            in_specs=[pl.BlockSpec((strip * rows // pieces, depth), lambda i, p: (i, 0))]
            + [WHOLE] * len(weights),
            out_specs=pl.BlockSpec((strip, rows // pieces, width), lambda i, p: (i, 0, 0)),
        ),
        out_shape=jax.ShapeDtypeStruct((pieces, rows // pieces, width), jnp.bfloat16),
        compiler_params=pltpu.CompilerParams(vmem_limit_bytes=55 * 1024 * 1024),
        cost_estimate=BRIEF,
    )(place, tokens, *weights)


def assemble_kernel(first, part, *refs):
    out, left = refs[-2:]
    count, _, width = part.shape
    sent = []
    for j in range(count):
        for s in range(width // LANES):
            column = (first + s) * count + j
            sent.append(
                pltpu.make_async_copy(
                    part.at[j, :, pl.ds(s * LANES, LANES)],
                    out.at[:, pl.ds(column * LANES, LANES)],
                    left.at[j, s],
                )
            )
    for copy in sent:
        copy.start()
    for copy in sent:
        copy.wait()


def assemble(part, whole, first):
    count, rows, width = part.shape
    held = [] if whole is None else [whole]
    return pl.pallas_call(
        functools.partial(assemble_kernel, first),
        in_specs=[WHOLE] + [ANYWHERE] * len(held),
        out_specs=ANYWHERE,
        out_shape=jax.ShapeDtypeStruct((rows, SLICES * count * LANES), jnp.bfloat16),
        scratch_shapes=[pltpu.SemaphoreType.DMA((count, width // LANES))],
        input_output_aliases={1: 0} if held else {},
        compiler_params=pltpu.CompilerParams(vmem_limit_bytes=16 * 1024 * 1024),
        cost_estimate=BRIEF,
    )(part, *held)


def ring(array, axis):
    n = lax.axis_size(axis)
    pairs = [(2 * i + c, 2 * ((i + 1 - 2 * c) % n) + c) for i in range(n) for c in (0, 1)]
    return lax.ppermute(array, (axis, "c"), pairs)


def rings(block):
    blocks = [block]
    for _ in range(lax.axis_size("zh") - 1):
        blocks.append(ring(blocks[-1], "zh"))
    return blocks


def after(array, *earlier):
    return lax.optimization_barrier((array, earlier))[0]


def body(
    inner_weights, inner_grads, first_moment, second_moment, anchor, outer_momentum, next_tokens
):
    groups = lax.axis_size(GROUP)
    place = lax.axis_index(GROUP).astype(jnp.int32).reshape(1)
    turn = 2 * lax.axis_index("c") - 1
    deep = next_tokens.shape[1] // lax.axis_size("zh")
    spot = [
        (lax.axis_index("zh") + turn * k) % lax.axis_size("zh") * deep + half
        for half in (0, deep // 2)
        for k in range(4)
    ]
    spot = jnp.stack(spot).astype(jnp.int32)
    anchor = anchor.transpose(1, 0, 2)
    momentum = outer_momentum.transpose(1, 0, 2)
    state = (inner_weights[0], inner_grads[0], first_moment[0], second_moment[0], anchor)

    pieces, anchor_part = inner_step(place, *state, groups)
    pieces = lax.all_to_all(pieces, GROUP, 0, 0, tiled=True)
    anchor_new, momentum_new, mixed = outer_step(pieces, anchor_part, momentum)
    tokens = lax.all_gather(next_tokens, PLANE, axis=0, tiled=True)
    mixed = lax.all_to_all(mixed, GROUP, 0, 0, tiled=True)
    mixed = lax.all_to_all(mixed, PLANE, 0, 0, tiled=True)
    block = mixed.reshape(-1, mixed.shape[2])
    half = block.shape[0] // 2
    low, high = block[:half], block[half:]
    cut = CUT * LANES
    low_a, high_a = rings(low[:, :cut]), rings(high[:, :cut])
    low_b, high_b = rings(after(low[:, cut:], low_a[:3])), rings(after(high[:, cut:], high_a[:3]))
    out_a = product(spot, tokens, low_a + high_a, lax.axis_size(PLANE), 4)
    out_a = after(out_a, low_b[1], high_b[1])
    part_a = lax.all_to_all(out_a, PLANE, 0, 0, tiled=True)
    out_b = product(spot, tokens, low_b + high_b, lax.axis_size(PLANE), 2)
    part_b = lax.all_to_all(out_b, PLANE, 0, 0, tiled=True)
    preactivations = assemble(part_a, None, 0)
    preactivations = assemble(part_b, preactivations, CUT)
    return (preactivations, anchor_new.transpose(1, 0, 2), momentum_new.transpose(1, 0, 2))


def solution(mesh):
    fine = Mesh(mesh.devices.reshape(2, 4, 4, 4, 2), GROUP + ROWS)
    shard = P(GROUP, ROWS, None)
    in_specs = (
        shard,
        shard,
        shard,
        shard,
        P(ROWS, None, None),
        P(ROWS, None, GROUP),
        P(GROUP + ROWS, None),
    )
    out_specs = (P(GROUP + ROWS, None), P(ROWS, None, GROUP), P(ROWS, None, GROUP))
    return jax.shard_map(body, mesh=fine, in_specs=in_specs, out_specs=out_specs, check_vma=False)
```
